32 devices in a mesh: az: 4 (over y, core), rg: 8 (over z, x).
Axes of the slice: x: 2, y: 2, z: 4, core: 2. Of those that a mesh axis runs over, the one named last changes fastest.
Arguments:
- master_raw: float32 [2, 2048, 20000], P(None, 'az', 'rg'), may hold values from -6 to 6
- slave_raw: float32 [2, 2048, 20000], P(None, 'az', 'rg'), may hold values from -6 to 6
- range_ref: float32 [2, 20000], replicated, may hold values from -4 to 4
- az_ref: float32 [2, 2048], replicated, may hold values from -4 to 4
- az_shift: int32 [4, 256], P(None, ('az', 'rg')), may hold values from -32 to 32, as said below
- rg_shift: int32 [4, 256], P(None, ('az', 'rg')), may hold values from -64 to 64, as said below
- valid_lines: int32 [256], replicated, may hold values from 1024 to 2048, as said below
Outputs:
- interferogram: float32 [2, 256, 2048], P(None, None, ('az', 'rg'))
The draws below stay inside these ranges and needn't reach their ends.
Inputs may be any that keep to these rules, and one draw needn't show every extreme that they name: `az_shift`: azimuth offset of the slave in lines for each block of 512 lines and 64 samples. `rg_shift`: range offset of the slave in samples for each block of 512 lines and 64 samples. Lines 0 to valid_lines[t] - 1 of range tile t are valid.
All inputs are finite; a program needn't handle non-finite values.
Results may differ from the reference program's by a relative error of at most 0.0003.
Values sent between devices are 32-bit elements; how exact they have to be, the bound alone decides.
A program may use at most 512 MiB of HBM per device.

```python
import jax
import jax.numpy as jnp
from jax import lax

LINES = 2048
RANGE = 20000
RV = 16384
LOOK = 8
BA = 512
BR = 64
ASH = 32
RSH = 64
NBA = 4
NBR = 256


def forced_table(key, count, lowest, highest):
    key_values, key_first, key_second = jax.random.split(key, 3)
    values = jax.random.randint(key_values, (count,), lowest, highest + 1)
    index_first = jax.random.randint(key_first, (), 0, count)
    index_second = (index_first + 1 + jax.random.randint(key_second, (), 0, count - 1)) % count
    return values.at[index_first].set(highest).at[index_second].set(lowest).astype(jnp.int32)


def draw_az_shift(key, part):
    return forced_table(jax.random.fold_in(key, 101), NBA * NBR, -ASH, ASH).reshape(NBA, NBR)


def draw_rg_shift(key, part):
    return forced_table(jax.random.fold_in(key, 202), NBA * NBR, -RSH, RSH).reshape(NBA, NBR)


def draw_valid_lines(key, part):
    return forced_table(jax.random.fold_in(key, 303), NBR, LINES // 2, LINES)


def level_of(rng, dims, cuts, smallest, high):
    gain = 1.0
    for axis_at, shards_of in cuts:
        draws = jax.random.uniform(jax.random.fold_in(jax.random.fold_in(rng, 6), axis_at), (shards_of,), jnp.float32, smallest / len(cuts), high / len(cuts))
        gain = gain * jnp.repeat(jnp.exp(draws), dims[axis_at] // shards_of).reshape((-1,) + (1,) * (len(dims) - 1 - axis_at))
    return gain


def bell_draw(own_key, extent, width, limit, cuts=(), kind=jnp.bfloat16):
    loudness = level_of(own_key, extent, cuts, -0.22, 0.18) if cuts else 1.0
    values = jax.random.normal(own_key, extent, jnp.float32) * width * loudness
    return jnp.minimum(jnp.maximum(values, -limit), limit).astype(kind)


def setup_inputs(seed: int = 0) -> dict:
    streams_of = jax.random.split(jax.random.key(seed), 8)
    master_raw = bell_draw(streams_of[0], (2, LINES, RANGE), 1.0, 6.0, ((1, 4), (2, 8)), jnp.float32)
    slave_raw = bell_draw(streams_of[1], (2, LINES, RANGE), 1.0, 6.0, ((1, 4), (2, 8)), jnp.float32)
    range_ref = bell_draw(streams_of[2], (2, RANGE), 0.6, 4.0, (), jnp.float32)
    az_ref = bell_draw(streams_of[3], (2, LINES), 0.6, 4.0, (), jnp.float32)
    az_shift = draw_az_shift(jax.random.fold_in(streams_of[7], 71), 0)
    rg_shift = draw_rg_shift(jax.random.fold_in(streams_of[7], 71), 0)
    valid_lines = draw_valid_lines(jax.random.fold_in(streams_of[7], 71), 0)
    return dict(master_raw=master_raw, slave_raw=slave_raw, range_ref=range_ref, az_ref=az_ref, az_shift=az_shift, rg_shift=rg_shift, valid_lines=valid_lines)


def focus_image(raw_data, range_ref, az_ref):
    range_filter = range_ref[0] + 1j * range_ref[1]

    def range_block(block_index):
        line_start = (block_index * BA).astype(jnp.int32)
        block_data = lax.dynamic_slice_in_dim(raw_data, line_start, BA, 1)
        signal = block_data[0] + 1j * block_data[1]
        spectrum = jnp.fft.fft(signal, axis=1) * range_filter[None, :]
        return jnp.fft.ifft(spectrum, axis=1)[:, :RV]
    ranged = lax.map(range_block, jnp.arange(LINES // BA, dtype=jnp.int32)).reshape(LINES, RV)
    spectrum = jnp.fft.fft(ranged, axis=0) * (az_ref[0] + 1j * az_ref[1])[:, None]
    focused = jnp.fft.ifft(spectrum, axis=0)
    return (jnp.real(focused), jnp.imag(focused))

def resample(slave_field, az_shift, rg_shift):
    padded = jnp.pad(slave_field, ((0, 0), (ASH, ASH), (RSH, RSH)))
    row_start = (lax.broadcasted_iota(jnp.int32, (NBA, NBR), 0) * BA + ASH + az_shift).astype(jnp.int32)
    col_start = (lax.broadcasted_iota(jnp.int32, (NBA, NBR), 1) * BR + RSH + rg_shift).astype(jnp.int32)

    def cutout(row_begin, col_begin):
        return lax.dynamic_slice(padded, (jnp.int32(0), row_begin, col_begin), (2, BA, BR))
    pieces = jax.vmap(jax.vmap(cutout))(row_start, col_start)
    return pieces.transpose(2, 0, 3, 1, 4).reshape(2, LINES, RV)

def box_filter(padded_grid, rows_out, cols_out):
    total = padded_grid[..., 0:rows_out, 0:cols_out]
    for row_step in range(3):
        for col_step in range(3):
            if row_step + col_step > 0:
                total = total + padded_grid[..., row_step:row_step + rows_out, col_step:col_step + cols_out]
    return total

def reference(master_raw, slave_raw, range_ref, az_ref, az_shift, rg_shift, valid_lines):
    master_real, master_imag = focus_image(master_raw, range_ref, az_ref)
    slave_real, slave_imag = focus_image(slave_raw, range_ref, az_ref)
    moved = resample(jnp.stack([slave_real, slave_imag]), az_shift, rg_shift)
    col_counts = jnp.repeat(valid_lines, BR)
    valid_mask = (lax.broadcasted_iota(jnp.int32, (LINES, RV), 0) < col_counts[None, :]).astype(master_real.dtype)
    cross_real = (master_real * moved[0] + master_imag * moved[1]) * valid_mask
    cross_imag = (master_imag * moved[0] - master_real * moved[1]) * valid_mask
    rows_out = LINES // LOOK
    cols_out = RV // LOOK
    looks = jnp.stack([cross_real, cross_imag]).reshape(2, rows_out, LOOK, cols_out, LOOK).sum(axis=(2, 4))
    groups = lax.broadcasted_iota(jnp.int32, (rows_out, cols_out), 0)
    look_counts = jnp.repeat(valid_lines, BR // LOOK)
    pixels = (jnp.clip(look_counts[None, :] - LOOK * groups, 0, LOOK) * LOOK).astype(master_real.dtype)
    box = box_filter(jnp.pad(looks, ((0, 0), (1, 1), (1, 1))), rows_out, cols_out)
    box_pixels = box_filter(jnp.pad(pixels, ((1, 1), (1, 1))), rows_out, cols_out)
    return box / jnp.sqrt(jnp.maximum(box_pixels, 1.0))[None]
```

```python
from functools import partial
import math

import jax
import jax.numpy as jnp
import numpy as np
from jax import lax
from jax.experimental import pallas as pl
from jax.experimental.pallas import tpu as pltpu
from jax.sharding import PartitionSpec as P

RV = 16384
LOOK = 8
BA = 512
BR = 64
ASH = 32
RSH = 64
LANES = 128
RN1 = 200
RN2 = 100
RPAD = 104
MCHUNK = 8
F32 = jnp.float32
BF16 = jnp.bfloat16


def real_form(table):
    return np.block([[table.real, -table.imag], [table.imag, table.real]])


def split_table(table):
    high = table.astype(BF16)
    low = (table - high.astype(np.float64)).astype(BF16)
    return np.concatenate([high, low, high], axis=1)


def unit(product, length, sign):
    return np.exp(sign * 2j * np.pi * (product % length) / length)


def split_value(value):
    high = value.astype(BF16)
    return high, (value - high.astype(F32)).astype(BF16)


def stacked(value):
    high, low = split_value(value)
    return jnp.concatenate([high, high, low], axis=0)


def dot(a, b):
    return jnp.dot(a, b, preferred_element_type=F32)


def middle_matrices(reference, outer, inner, pad):
    length = outer * inner
    k, n = np.arange(outer), np.arange(inner)
    turn = np.zeros((inner, pad, pad), np.complex128)
    turn[:, :inner, :inner] = unit(
        n[:, None, None] * (n[None, :, None] - n[None, None, :]), inner, 1
    ) / length
    spec = (reference[0].reshape(inner, outer).T, reference[1].reshape(inner, outer).T)
    contract = partial(
        jnp.einsum, "kj,jmn->kmn", precision=lax.Precision.HIGHEST, preferred_element_type=F32
    )
    t_re, t_im = jnp.asarray(turn.real, F32), jnp.asarray(turn.imag, F32)
    h_re = contract(spec[0], t_re) - contract(spec[1], t_im)
    h_im = contract(spec[0], t_im) + contract(spec[1], t_re)
    ang = unit(k[:, None] * n[None, :], length, 1)
    thin = np.zeros((outer, pad), np.complex128)
    thin[:, :inner] = ang
    a_re, a_im = jnp.asarray(thin.real, F32), jnp.asarray(thin.imag, F32)
    w_re = a_re[:, :, None] * a_re[:, None, :] + a_im[:, :, None] * a_im[:, None, :]
    w_im = a_im[:, :, None] * a_re[:, None, :] - a_re[:, :, None] * a_im[:, None, :]
    m_re = h_re * w_re - h_im * w_im
    m_im = h_re * w_im + h_im * w_re
    top = jnp.concatenate([m_re, -m_im], axis=2)
    low = jnp.concatenate([m_im, m_re], axis=2)
    return jnp.concatenate([top, low], axis=1)


def azimuth_kernel(outer, inner, sources, dests, x_ref, f_ref, g_ref, m_ref, o_ref, z_ref):
    per_source = outer // sources
    group = outer // dests
    for q in range(0, inner, 2):
        halves = []
        for s in range(2):
            halves.append(
                jnp.concatenate(
                    [
                        x_ref[a, c, pl.ds(q + s, per_source, stride=inner), :]
                        for a in range(sources)
                        for c in range(2)
                    ],
                    axis=0,
                )
            )
        y = dot(f_ref[...], stacked(jnp.concatenate(halves, axis=1)))
        for s in range(2):
            for c in range(2):
                z_ref[pl.ds(c * inner + q + s, outer, stride=2 * inner), :] = y[
                    c * outer : (c + 1) * outer, s * LANES : (s + 1) * LANES
                ]

    def middle(k, _):
        at = pl.ds(pl.multiple_of(k * (2 * inner), 2 * inner), 2 * inner)
        high, low = split_value(z_ref[at, :])
        m_high, m_low = split_value(m_ref[k])
        both = dot(m_high, jnp.concatenate([high, low], axis=1))
        z_ref[at, :] = both[:, :LANES] + both[:, LANES:] + dot(m_low, high)
        return 0

    lax.fori_loop(0, outer, middle, 0, unroll=8)
    for q in range(0, inner, 2):
        halves = []
        for s in range(2):
            halves.append(
                jnp.concatenate(
                    [
                        z_ref[pl.ds(c * inner + q + s, outer, stride=2 * inner), :]
                        for c in range(2)
                    ],
                    axis=0,
                )
            )
        y = dot(g_ref[...], stacked(jnp.concatenate(halves, axis=1)))
        for s in range(2):
            for c in range(2):
                for g in range(group):
                    row = (c * group + g) * dests
                    o_ref[pl.ds(c * group * inner + g * inner + q + s, dests, stride=2 * group * inner), :] = y[
                        row : row + dests, s * LANES : (s + 1) * LANES
                    ]


def azimuth_compress(field, matrices, devices, order):
    sources, _, lines_here, columns = field.shape
    lines = sources * lines_here
    lines_each = lines // devices
    inner = min(32, lines_each)
    outer = lines // inner
    group = lines_each // inner
    p = np.arange(outer)
    forward = real_form(unit(p[:, None] * p[None, :], outer, -1))
    backward = real_form(unit(p[:, None] * p[None, :], outer, 1))
    cols = np.array(
        [
            c * outer + a * (outer // sources) + i
            for a in range(sources)
            for c in range(2)
            for i in range(outer // sources)
        ]
    )
    rows = np.array(
        [c * outer + d * group + g for c in range(2) for g in range(group) for d in order]
    )
    forward = split_table(forward[:, cols])
    backward = split_table(backward[rows])
    wide = pl.cdiv(columns, LANES)
    out = pl.pallas_call(
        partial(azimuth_kernel, outer, inner, sources, devices),
        grid=(wide,),
        in_specs=[
            pl.BlockSpec((sources, 2, lines_here, LANES), lambda i: (0, 0, 0, i)),
            pl.BlockSpec(forward.shape, lambda i: (0, 0)),
            pl.BlockSpec(backward.shape, lambda i: (0, 0)),
            pl.BlockSpec(matrices.shape, lambda i: (0, 0, 0)),
        ],
        out_specs=pl.BlockSpec((2 * lines, LANES), lambda i: (0, i)),
        out_shape=jax.ShapeDtypeStruct((2 * lines, columns), F32),
        scratch_shapes=[pltpu.VMEM((2 * lines, LANES), F32)],
        compiler_params=pltpu.CompilerParams(vmem_limit_bytes=48 * 1024 * 1024),
        cost_estimate=pl.CostEstimate(
            flops=12 * wide * LANES * lines * (4 * outer + 2 * inner),
            bytes_accessed=16 * lines * columns,
            transcendentals=0,
        ),
        name="azimuth",
    )(field, jnp.asarray(forward), jnp.asarray(backward), matrices)
    return out.reshape(devices, 2, lines_each, columns)


def range_kernel(keep, x_ref, f_ref, g_ref, m_ref, o_ref, buf, z_ref, m_buf, sem, m_sem):
    def fetch(i, slot):
        return pltpu.make_async_copy(
            m_ref.at[pl.ds(i * MCHUNK, MCHUNK)], m_buf.at[slot], m_sem.at[slot]
        )

    load = pltpu.make_async_copy(x_ref, buf, sem.at[0])
    load.start()
    fetch(0, 0).start()
    load.wait()
    zero = jnp.zeros((RPAD - RN2, LANES), F32)

    def clear(k, _):
        for c in range(2):
            z_ref[k, c, pl.ds(RN2, RPAD - RN2), :] = zero
        return 0

    lax.fori_loop(0, RN1, clear, 0, unroll=8)

    def first(i, _):
        halves = []
        for s in range(2):
            halves.append(
                jnp.concatenate(
                    [buf[c, pl.ds(2 * i + s, RN1, stride=RN2), :] for c in range(2)], axis=0
                )
            )
        y = dot(f_ref[...], stacked(jnp.concatenate(halves, axis=1)))
        for s in range(2):
            for c in range(2):
                z_ref[:, c, 2 * i + s, :] = y[
                    c * RN1 : (c + 1) * RN1, s * LANES : (s + 1) * LANES
                ]
        return 0

    lax.fori_loop(0, RN2 // 2, first, 0)

    def middle(i, _):
        slot = lax.rem(i, 2)

        @pl.when(i + 1 < RN1 // MCHUNK)
        def _():
            fetch(i + 1, 1 - slot).start()

        fetch(i, slot).wait()
        for j in range(MCHUNK):
            k = i * MCHUNK + j
            high, low = split_value(z_ref[k].reshape(2 * RPAD, LANES))
            m_high, m_low = split_value(m_buf[slot, j])
            both = dot(m_high, jnp.concatenate([high, low], axis=1))
            y = both[:, :LANES] + both[:, LANES:] + dot(m_low, high)
            z_ref[k] = y.reshape(2, RPAD, LANES)
        return 0

    lax.fori_loop(0, RN1 // MCHUNK, middle, 0)

    def last(i, _):
        halves = []
        for s in range(2):
            halves.append(
                jnp.concatenate([z_ref[:, c, 2 * i + s, :] for c in range(2)], axis=0)
            )
        y = dot(g_ref[...], stacked(jnp.concatenate(halves, axis=1)))
        for s in range(2):
            for c in range(2):
                buf[c, pl.ds(2 * i + s, keep, stride=RN2), :] = y[
                    c * keep : (c + 1) * keep, s * LANES : (s + 1) * LANES
                ]
        return 0

    lax.fori_loop(0, RN2 // 2, last, 0)
    store = pltpu.make_async_copy(buf.at[:, pl.ds(0, RV), :], o_ref, sem.at[0])
    store.start()
    store.wait()


def range_compress(field, matrices):
    length = field.shape[1]
    keep = -(-RV // RN2)
    keep += -keep % 8
    n = np.arange(RN1)
    forward = split_table(real_form(unit(n[:, None] * n[None, :], RN1, -1)))
    backward = split_table(real_form(unit(n[:keep, None] * n[None, :], RN1, 1)))
    return pl.pallas_call(
        partial(range_kernel, keep),
        in_specs=[
            pl.BlockSpec(memory_space=pl.ANY),
            pl.BlockSpec(memory_space=pltpu.VMEM),
            pl.BlockSpec(memory_space=pltpu.VMEM),
            pl.BlockSpec(memory_space=pl.ANY),
        ],
        out_specs=pl.BlockSpec(memory_space=pl.ANY),
        out_shape=jax.ShapeDtypeStruct((2, RV, LANES), F32),
        scratch_shapes=[
            pltpu.VMEM((2, length, LANES), F32),
            pltpu.VMEM((RN1, 2, RPAD, LANES), F32),
            pltpu.VMEM((2, MCHUNK, 2 * RPAD, 2 * RPAD), F32),
            pltpu.SemaphoreType.DMA((1,)),
            pltpu.SemaphoreType.DMA((2,)),
        ],
        compiler_params=pltpu.CompilerParams(vmem_limit_bytes=58 * 1024 * 1024),
        cost_estimate=pl.CostEstimate(
            flops=12 * LANES * length * (4 * RN1 + 2 * RN2),
            bytes_accessed=100 * 1024 * 1024,
            transcendentals=0,
        ),
        name="range",
    )(field, jnp.asarray(forward), jnp.asarray(backward), matrices)


def cross_kernel(line_count, az_ref, rg_ref, valid_ref, first_ref, m_ref, s_ref, o_ref):
    first = first_ref[0]
    lane = lax.broadcasted_iota(jnp.int32, (BR, LANES), 1)

    def tile(t, _):
        start = RSH + t * BR + rg_ref[t]
        turn = lax.rem(LANES - ASH - az_ref[t], LANES)
        moved = [
            pltpu.roll(s_ref[c, pl.ds(start, BR), :], turn, 1) for c in range(2)
        ]
        at = pl.ds(pl.multiple_of(t * BR, BR), BR)
        real, imag = m_ref[0, at, :], m_ref[1, at, :]
        shown = (lane + first < valid_ref[t]) & (lane < line_count)
        cross = (
            real * moved[0] + imag * moved[1],
            imag * moved[0] - real * moved[1],
        )
        for c in range(2):
            kept = jnp.where(shown, cross[c], 0.0)
            o_ref[c, pl.ds(pl.multiple_of(t * LOOK, LOOK), LOOK), :] = kept.reshape(
                BR // LOOK, LOOK, LANES
            ).sum(axis=1)
        return 0

    lax.fori_loop(0, RV // BR, tile, 0, unroll=2)


def cross_looks(focused, window, az_row, rg_row, valid_lines, first, line_count):
    smem = pl.BlockSpec(memory_space=pltpu.SMEM)
    vmem = pl.BlockSpec(memory_space=pltpu.VMEM)
    return pl.pallas_call(
        partial(cross_kernel, line_count),
        in_specs=[smem, smem, smem, smem, vmem, vmem],
        out_specs=vmem,
        out_shape=jax.ShapeDtypeStruct((2, RV // LOOK, LANES), F32),
        compiler_params=pltpu.CompilerParams(vmem_limit_bytes=48 * 1024 * 1024),
        cost_estimate=pl.CostEstimate(
            flops=16 * RV * LANES, bytes_accessed=36 * 1024 * 1024, transcendentals=0
        ),
        name="cross",
    )(az_row, rg_row, valid_lines, first, focused, window)


def box_filter(padded_grid, rows_out, cols_out):
    total = padded_grid[..., 0:rows_out, 0:cols_out]
    for row_step in range(3):
        for col_step in range(3):
            if row_step + col_step > 0:
                total = (
                    total
                    + padded_grid[
                        ..., row_step : row_step + rows_out, col_step : col_step + cols_out
                    ]
                )
    return total


def local(master_raw, slave_raw, range_ref, az_ref, az_shift, rg_shift, valid_lines):
    both = ("az", "rg")
    az_count = lax.axis_size("az")
    rg_count = lax.axis_size("rg")
    devices = az_count * rg_count
    lines_here, samples = master_raw.shape[1:]
    lines = lines_here * az_count
    length = samples * rg_count
    lines_each = lines // devices
    az_index = lax.axis_index("az")
    rg_index = lax.axis_index("rg")
    place = rg_index * az_count + az_index
    order = [r * az_count + a for a in range(az_count) for r in range(rg_count)]
    share = -(-samples // az_count)
    share += -share % 32

    az_inner = min(32, lines_each)
    az_mid = middle_matrices(az_ref, lines // az_inner, az_inner, az_inner)
    range_mid = middle_matrices(range_ref, RN1, RN2, RPAD)

    def focus_lines(raw):
        padded = jnp.pad(raw, ((0, 0), (0, 0), (0, share * az_count - samples)))
        parts = padded.reshape(2, lines_here, az_count, share).transpose(2, 0, 1, 3)
        turned = lax.all_to_all(parts, "az", split_axis=0, concat_axis=0, tiled=True)
        done = azimuth_compress(turned, az_mid, devices, order)
        return lax.all_to_all(done, both, split_axis=0, concat_axis=0, tiled=True)

    def columns_first(field):
        field = field.reshape(az_count, rg_count, 2, lines_each, share)
        field = field.transpose(2, 1, 0, 4, 3).reshape(2, rg_count, az_count * share, lines_each)
        return field[:, :, :samples].reshape(2, length, lines_each)

    images = [columns_first(focus_lines(raw)) for raw in (master_raw, slave_raw)]
    pair = jnp.concatenate(images, axis=2)
    pair = jnp.pad(pair, ((0, 0), (0, 0), (0, LANES - 2 * lines_each)))
    focused = range_compress(pair, range_mid)
    slave = focused[:, :, lines_each : 2 * lines_each]

    chain = [(i % az_count) * rg_count + i // az_count for i in range(devices)]
    reach = min(ASH, lines_each)
    before, after = [], []
    for hop in range(1, ASH // reach + 1):
        up = [(chain[i], chain[i + hop]) for i in range(devices - hop)]
        down = [(j, i) for i, j in up]
        before.insert(0, lax.ppermute(slave[:, :, lines_each - reach :], both, up))
        after.append(lax.ppermute(slave[:, :, :reach], both, down))
    window = jnp.concatenate(before + [slave] + after, axis=2)
    window = jnp.pad(window, ((0, 0), (RSH, RSH), (0, LANES - window.shape[2])))

    first = place * lines_each
    block = first // BA
    shifts = lax.all_gather(jnp.stack([az_shift, rg_shift]), both, axis=2, tiled=True)
    rows = lax.dynamic_index_in_dim(shifts, block, axis=1, keepdims=False)
    sums = cross_looks(
        focused, window, rows[0], rows[1], valid_lines, first.reshape(1), lines_each
    )
    rows_each = lines_each // LOOK
    cols_all = RV // LOOK
    looks = sums[:, :, :lines_each].reshape(2, cols_all, rows_each, LOOK).sum(axis=3)

    rows_out = lines // LOOK
    cols_out = cols_all // devices
    wide = jnp.pad(looks, ((0, 0), (1, 1), (0, 0)))
    inside = looks.reshape(2, devices, cols_out, rows_each)
    left = wide[:, :cols_all].reshape(2, devices, cols_out, rows_each)[:, :, :1]
    right = wide[:, 2:].reshape(2, devices, cols_out, rows_each)[:, :, -1:]
    sent = jnp.concatenate([left, inside, right], axis=2).transpose(1, 0, 2, 3)
    got = lax.all_to_all(sent, both, split_axis=0, concat_axis=0, tiled=True)
    got = got.reshape(az_count, rg_count, 2, cols_out + 2, rows_each)
    wide_looks = got.transpose(2, 1, 0, 4, 3).reshape(2, rows_out, cols_out + 2)

    blocks_here = valid_lines.shape[0] // devices
    flat_index = lax.axis_index(both)
    local_counts = lax.dynamic_slice(
        jnp.pad(valid_lines, 1), (flat_index * blocks_here,), (blocks_here + 2,)
    )
    wide_counts = jnp.concatenate(
        [local_counts[:1], jnp.repeat(local_counts[1:-1], BR // LOOK), local_counts[-1:]]
    )
    groups = lax.broadcasted_iota(jnp.int32, (rows_out, cols_out + 2), 0)
    pixels = (jnp.clip(wide_counts[None, :] - LOOK * groups, 0, LOOK) * LOOK).astype(F32)
    box = box_filter(jnp.pad(wide_looks, ((0, 0), (1, 1), (0, 0))), rows_out, cols_out)
    box_pixels = box_filter(jnp.pad(pixels, ((1, 1), (0, 0))), rows_out, cols_out)
    return box / jnp.sqrt(jnp.maximum(box_pixels, 1.0))[None]


def solution(mesh):
    return jax.shard_map(
        local,
        mesh=mesh,
        in_specs=(
            P(None, "az", "rg"),
            P(None, "az", "rg"),
            P(),
            P(),
            P(None, ("az", "rg")),
            P(None, ("az", "rg")),
            P(),
        ),
        out_specs=P(None, None, ("az", "rg")),
        check_vma=False,
    )
```
